32 devices in a mesh: ta: 4 (over x, core), ha: 4 (over z), hd: 2 (over y).
Axes of the slice: x: 2, y: 2, z: 4, core: 2. Of those that a mesh axis runs over, the one named last changes fastest.
Arguments:
- qkv: bfloat16 [16, 16, 64, 9216], P('ta', 'ha', 'hd'), may hold values from -40 to 40, as said below
- q_gain: float32 [128], replicated, may hold values from 0.5 to 4.5
- k_gain: float32 [128], replicated, may hold values from 0.5 to 4.5
- windows: int32 [24, 3], P('hd'), may hold values from 0 to 1, as said below
- frame_counts: int32 [8], replicated, may hold values from 1 to 2, as said below
- row_counts: int32 [8], replicated, may hold values from 1 to 2, as said below
Outputs:
- attended: bfloat16 [16, 16, 64, 3072], P('ta', 'ha', 'hd')
The draws below stay inside these ranges and needn't reach their ends.
Inputs may be any that keep to these rules, and one draw needn't show every extreme that they name: `qkv`: the last dimension holds the query, then the key, then the value, each as 24 heads of 128 entries. `windows`: every column reaches 1 for some head. `frame_counts`: some tile holds 2 frames. `row_counts`: some tile holds 2 rows.
All inputs are finite; a program needn't handle non-finite values.
Results may differ from the reference program's by a relative error of at most 0.012.
The reference program's roundings to bfloat16 on the way (of `weights`) count: a program that leaves them out, or rounds other values in their place, can miss the bound.
Values may be sent and summed in bfloat16 or wider, within the bound.
A program may use at most 128 MiB of HBM per device.

```python
import math
import jax
import jax.numpy as jnp
from jax import lax

HEADS = 24
HEAD_DIM = 128
TT = 2
TH = 2
TW = 8
COLS = 64
FRAMES = 16
ROWS = 16
TILES_T = 8
TILES_H = 8


def draw_qkv(key, part):
    layout = (FRAMES, ROWS, COLS, 3, HEADS, HEAD_DIM)
    values = jnp.clip(jax.random.normal(jax.random.fold_in(key, 1), layout, jnp.float32), -6.0, 6.0)
    return values.reshape(FRAMES, ROWS, COLS, 3 * HEADS * HEAD_DIM).astype(jnp.bfloat16)


def draw_q_gain(key, part):
    values = jnp.exp(jax.random.uniform(jax.random.fold_in(key, 62), (HEAD_DIM,), jnp.float32, math.log(0.5), math.log(2.0)))
    return values.astype(jnp.float32)


def draw_k_gain(key, part):
    values = jnp.exp(jax.random.uniform(jax.random.fold_in(key, 72), (HEAD_DIM,), jnp.float32, math.log(0.5), math.log(2.0)))
    return values.astype(jnp.float32)


def draw_windows(key, part):
    radius = jax.random.randint(jax.random.fold_in(key, 21), (HEADS, 3), 0, 2)
    forced = jax.random.randint(jax.random.fold_in(key, 22), (1, 3), 0, HEADS)
    return jnp.where(jnp.arange(HEADS)[:, None] == forced, 1, radius).astype(jnp.int32)


def count_tables(key):
    base = jax.random.fold_in(key, 30)
    frames = jax.random.randint(jax.random.fold_in(base, 1), (TILES_T,), 1, TT + 1)
    frame_forced = jax.random.randint(jax.random.fold_in(base, 2), (), 0, TILES_T)
    frames = jnp.where(jnp.arange(TILES_T) == frame_forced, TT, frames)
    rows = jax.random.randint(jax.random.fold_in(base, 3), (TILES_H,), 1, TH + 1)
    spot = jax.random.randint(jax.random.fold_in(base, 4), (), 0, min(TILES_T, TILES_H))
    row_forced = (spot + 1 + jax.random.randint(jax.random.fold_in(base, 5), (), 0, TILES_H - 1)) % TILES_H
    frame_at = jnp.sum(jnp.where(jnp.arange(TILES_T) == spot, frames, 0))
    rows = jnp.where(jnp.arange(TILES_H) == spot, TH + 1 - frame_at, rows)
    rows = jnp.where(jnp.arange(TILES_H) == row_forced, TH, rows)
    return (frames.astype(jnp.int32), rows.astype(jnp.int32))


def draw_frame_counts(key, part):
    return count_tables(key)[0]


def draw_row_counts(key, part):
    return count_tables(key)[1]


def setup_inputs(seed: int = 0) -> dict:
    keys = jax.random.split(jax.random.key(seed), 7)
    qkv = draw_qkv(jax.random.fold_in(keys[6], 71), 0)
    q_gain = draw_q_gain(jax.random.fold_in(keys[6], 71), 0)
    k_gain = draw_k_gain(jax.random.fold_in(keys[6], 71), 0)
    windows = draw_windows(jax.random.fold_in(keys[6], 71), 0)
    frame_counts = draw_frame_counts(jax.random.fold_in(keys[6], 71), 0)
    row_counts = draw_row_counts(jax.random.fold_in(keys[6], 71), 0)
    return dict(qkv=qkv, q_gain=q_gain, k_gain=k_gain, windows=windows, frame_counts=frame_counts, row_counts=row_counts)


def normalize(part_values, gain):
    widened = part_values.astype(jnp.float32)
    meansq = lax.optimization_barrier(jnp.mean(widened * widened, axis=-1, keepdims=True))
    return (widened * lax.rsqrt(meansq + 1e-06) * gain).astype(jnp.bfloat16)

def valid_cells(position, extent, counts):
    tile_index = position // extent
    listed = jnp.arange(counts.shape[0], dtype=jnp.int32)
    holding = lax.optimization_barrier(jnp.sum(jnp.where(tile_index[:, None] == listed[None, :], counts[None, :], 0), axis=1))
    return position % extent < holding

def reference(qkv, q_gain, k_gain, windows, frame_counts, row_counts):
    grouped = qkv.reshape(FRAMES, ROWS, COLS, 3, HEADS, HEAD_DIM)
    queries = normalize(grouped[:, :, :, 0], q_gain)
    widths = ((TT, TT), (TH, TH), (0, 0), (0, 0), (0, 0))
    keys_pad = jnp.pad(normalize(grouped[:, :, :, 1], k_gain), widths)
    values_pad = jnp.pad(grouped[:, :, :, 2], widths)
    col_tiles = jnp.arange(COLS, dtype=jnp.int32) // TW
    col_mask = jnp.abs(col_tiles[None, :, None] - col_tiles[None, None, :]) <= windows[:, 2, None, None]
    score_scale = 1.0 / math.sqrt(HEAD_DIM)

    def one_block(number):
        time_tile = number // TILES_H
        row_tile = number % TILES_H
        frame_start = (time_tile * TT).astype(jnp.int32)
        row_start = (row_tile * TH).astype(jnp.int32)
        zero = jnp.zeros((), jnp.int32)
        query_block = lax.dynamic_slice(queries, (frame_start, row_start, zero, zero, zero), (TT, TH, COLS, HEADS, HEAD_DIM)).reshape(-1, HEADS, HEAD_DIM)
        key_block = lax.dynamic_slice(keys_pad, (frame_start, row_start, zero, zero, zero), (3 * TT, 3 * TH, COLS, HEADS, HEAD_DIM)).reshape(-1, HEADS, HEAD_DIM)
        value_block = lax.dynamic_slice(values_pad, (frame_start, row_start, zero, zero, zero), (3 * TT, 3 * TH, COLS, HEADS, HEAD_DIM)).reshape(-1, HEADS, HEAD_DIM)
        query_frames = frame_start + jnp.arange(TT, dtype=jnp.int32)
        key_frames = frame_start - TT + jnp.arange(3 * TT, dtype=jnp.int32)
        query_rows = row_start + jnp.arange(TH, dtype=jnp.int32)
        key_rows = row_start - TH + jnp.arange(3 * TH, dtype=jnp.int32)
        time_mask = (jnp.abs(query_frames[None, :, None] // TT - key_frames[None, None, :] // TT) <= windows[:, 0, None, None]) & valid_cells(key_frames, TT, frame_counts)[None, None, :]
        row_mask = (jnp.abs(query_rows[None, :, None] // TH - key_rows[None, None, :] // TH) <= windows[:, 1, None, None]) & valid_cells(key_rows, TH, row_counts)[None, None, :]
        allowed = (time_mask[:, :, None, None, :, None, None] & row_mask[:, None, :, None, None, :, None] & col_mask[:, None, None, :, None, None, :]).reshape(HEADS, query_block.shape[0], key_block.shape[0])
        query_live = (valid_cells(query_frames, TT, frame_counts)[:, None, None] & valid_cells(query_rows, TH, row_counts)[None, :, None] & (col_tiles >= 0)[None, None, :]).reshape(-1)
        scores = jnp.einsum('qhd,khd->hqk', query_block.astype(jnp.float32), key_block.astype(jnp.float32)) * score_scale
        scores = jnp.where(allowed, scores, -1e+30)
        highest = lax.optimization_barrier(jnp.max(scores, axis=2, keepdims=True))
        raised = jnp.exp(scores - highest)
        summed = lax.optimization_barrier(jnp.sum(raised, axis=2, keepdims=True))
        weights = raised.astype(jnp.bfloat16)
        blended = jnp.einsum('hqk,khd->qhd', weights.astype(jnp.float32), value_block.astype(jnp.float32))
        result = jnp.where(query_live[:, None, None], blended / summed.transpose(1, 0, 2), 0.0)
        return result.astype(jnp.bfloat16)
    blocks = lax.map(one_block, jnp.arange(TILES_T * TILES_H, dtype=jnp.int32))
    blocks = blocks.reshape(TILES_T, TILES_H, TT, TH, COLS, HEADS, HEAD_DIM)
    return blocks.transpose(0, 2, 1, 3, 4, 5, 6).reshape(FRAMES, ROWS, COLS, HEADS * HEAD_DIM)
```

```python
import functools
import math

import jax
import jax.numpy as jnp
import numpy as np
from jax import lax
from jax.experimental import pallas as pl
from jax.experimental.pallas import tpu as pltpu
from jax.sharding import PartitionSpec as P

TT = 2
TH = 2
TW = 8


def extended(value, sides, width):
    for axis, dim in sides:
        size, length = (lax.axis_size(axis), value.shape[dim])
        up = [(i, (i + 1) % size) for i in range(size - 1)]
        down = [(j, i) for i, j in up]
        last = lax.slice_in_dim(value, length - width, length, axis=dim)
        initial = lax.slice_in_dim(value, 0, width, axis=dim)
        before = lax.ppermute(last, axis, up)
        after = lax.ppermute(initial, axis, down)
        value = jnp.concatenate([before, value, after], axis=dim)
    return value


def normalize(part_values, gain):
    widened = part_values.astype(jnp.float32)
    meansq = jnp.mean(widened * widened, axis=-1, keepdims=True)
    return (widened * lax.rsqrt(meansq + 1e-06) * gain).astype(jnp.bfloat16)


def valid_cells(position, extent, counts):
    tile_index = position // extent
    listed = jnp.arange(counts.shape[0], dtype=jnp.int32)
    holding = jnp.sum(jnp.where(tile_index[:, None] == listed[None, :], counts[None, :], 0), axis=1)
    return position % extent < holding


def extend_rims(paired):
    grown = extended(paired, (("ta", 0), ("ha", 1)), TT)
    return grown


def head_shards(qkv, q_gain, k_gain, windows, frame_counts, row_counts):
    frame_num, row_num, col_local, channels = qkv.shape
    head_dim = q_gain.shape[0]
    heads_all = channels // (3 * head_dim)
    sectioned = qkv.reshape(frame_num, row_num, col_local, 3, heads_all, head_dim)
    spread = lax.all_to_all(sectioned, "hd", split_axis=4, concat_axis=2, tiled=True)
    queries = normalize(spread[:, :, :, 0], q_gain)
    paired = jnp.stack([normalize(spread[:, :, :, 1], k_gain), spread[:, :, :, 2]], axis=3)
    padded = extend_rims(paired)
    col_num = queries.shape[2]
    heads_local = queries.shape[3]
    frame_base = lax.axis_index("ta") * frame_num
    row_base = lax.axis_index("ha") * row_num
    time_tiles = frame_num // TT
    score_scale = 1.0 / math.sqrt(head_dim)
    col_tiles = jnp.arange(col_num, dtype=jnp.int32) // TW
    col_gap = jnp.abs(col_tiles[:, None] - col_tiles[None, :])
    query_rows = row_base + jnp.arange(row_num, dtype=jnp.int32)
    key_rows = row_base - TH + jnp.arange(row_num + 2 * TH, dtype=jnp.int32)
    row_gap = jnp.abs(query_rows[:, None] // TH - key_rows[None, :] // TH)
    row_valid = valid_cells(key_rows, TH, row_counts)
    query_row_valid = valid_cells(query_rows, TH, row_counts)

    def attend(item_index):
        tile_at = item_index // heads_local
        head_at = item_index % heads_local
        first_frame = tile_at * TT
        query_block = lax.dynamic_slice(
            queries, (first_frame, 0, 0, head_at, 0), (TT, row_num, col_num, 1, head_dim)
        ).reshape(-1, head_dim)
        pair_block = lax.dynamic_slice(
            padded,
            (first_frame, 0, 0, 0, head_at, 0),
            (3 * TT, row_num + 2 * TH, col_num, 2, 1, head_dim),
        )
        key_block = pair_block[:, :, :, 0, 0].reshape(-1, head_dim)
        value_block = pair_block[:, :, :, 1, 0].reshape(-1, head_dim)
        radius = windows[head_at]
        query_frames = frame_base + first_frame + jnp.arange(TT, dtype=jnp.int32)
        key_frames = frame_base + first_frame - TT + jnp.arange(3 * TT, dtype=jnp.int32)
        time_mask = (
            jnp.abs(query_frames[:, None] // TT - key_frames[None, :] // TT) <= radius[0]
        ) & valid_cells(key_frames, TT, frame_counts)[None, :]
        row_mask = (row_gap <= radius[1]) & row_valid[None, :]
        col_mask = col_gap <= radius[2]
        allowed = (
            time_mask[:, None, None, :, None, None]
            & row_mask[None, :, None, None, :, None]
            & col_mask[None, None, :, None, None, :]
        ).reshape(query_block.shape[0], key_block.shape[0])
        query_live = (
            valid_cells(query_frames, TT, frame_counts)[:, None, None]
            & query_row_valid[None, :, None]
            & (col_tiles >= 0)[None, None, :]
        ).reshape(-1)
        scores = (
            jnp.einsum("qd,kd->qk", query_block, key_block, preferred_element_type=jnp.float32)
            * score_scale
        )
        scores = jnp.where(allowed, scores, -1e30)
        highest = jnp.max(scores, axis=1, keepdims=True)
        raised = jnp.exp(scores - highest)
        summed = jnp.sum(raised, axis=1, keepdims=True)
        weights = raised.astype(jnp.bfloat16)
        blended = jnp.dot(weights, value_block, preferred_element_type=jnp.float32)
        result = jnp.where(query_live[:, None], blended / summed, 0.0)
        return result.astype(jnp.bfloat16).reshape(TT, row_num, col_num, head_dim)

    outputs = lax.map(attend, jnp.arange(time_tiles * heads_local, dtype=jnp.int32))
    outputs = outputs.reshape(time_tiles, heads_local, TT, row_num, col_num, head_dim)
    outputs = outputs.transpose(0, 2, 3, 4, 1, 5).reshape(
        frame_num, row_num, col_num, heads_local, head_dim
    )
    gathered = lax.all_to_all(outputs, "hd", split_axis=2, concat_axis=3, tiled=True)
    return gathered.reshape(frame_num, row_num, col_local, heads_all * head_dim)


MASKED = -1e30
FEATURES = 128


def unit_rms(raw, gain):
    wide = raw.astype(jnp.float32)
    meansq = jnp.mean(wide * wide, axis=-1, keepdims=True)
    return (wide * lax.rsqrt(meansq + 1e-06) * gain).astype(jnp.bfloat16)


def attend_kernel(
    win, flive, rlive, q_ref, ke_ref, ve_ref, ky_ref, vy_ref, kfe_ref, kfy_ref, qf_ref,
    qg_ref, kg_ref, o_ref, qn, kn, kyn,
):
    frames, rows, cols, dim = q_ref.shape
    halo = ky_ref.shape[1] // (rows + 2 * TH)
    head = pl.program_id(0)
    w0, w1, w2 = win[head, 0], win[head, 1], win[head, 2]
    qg, kg = qg_ref[...], kg_ref[...]
    for f in range(frames):
        qn[f] = unit_rms(q_ref[f], qg)
    for f in range(frames + 2 * TT):
        kn[f] = unit_rms(ke_ref[f], kg)
        kyn[f] = unit_rms(ky_ref[f], kg)
    factor = math.log2(math.e) / math.sqrt(dim)

    def tile(t, r, near_t, near_r):
        fs = slice(t * TT + TT * (1 - near_t), t * TT + TT * (2 + near_t))
        r0, r1 = r * TH + TH * (1 - near_r), r * TH + TH * (2 + near_r)
        rs, ys = slice(r0, r1), slice(r0 * halo, r1 * halo)
        q = qn[t * TT : (t + 1) * TT, r * TH : (r + 1) * TH].reshape(-1, dim)
        q = jnp.concatenate([q, qf_ref[w2]], axis=1)
        nt = (((1,), (1,)), ((), ()))
        k1 = jnp.concatenate([kn[fs, rs].reshape(-1, dim), kfe_ref[fs, rs].reshape(-1, FEATURES)], axis=1)
        k2 = jnp.concatenate([kyn[fs, ys].reshape(-1, dim), kfy_ref[fs, ys].reshape(-1, FEATURES)], axis=1)
        s1 = lax.dot_general(q, k1, nt, preferred_element_type=jnp.float32)
        s2 = lax.dot_general(q, k2, nt, preferred_element_type=jnp.float32)
        top = jnp.maximum(jnp.max(s1, axis=1, keepdims=True), jnp.max(s2, axis=1, keepdims=True))
        p1 = jnp.exp2((s1 - top) * factor)
        p2 = jnp.exp2((s2 - top) * factor)
        summed = jnp.sum(p1, axis=1, keepdims=True) + jnp.sum(p2, axis=1, keepdims=True)
        v1 = ve_ref[fs, rs].reshape(-1, dim)
        v2 = vy_ref[fs, ys].reshape(-1, dim)
        out = jnp.dot(p1.astype(jnp.bfloat16), v1, preferred_element_type=jnp.float32)
        out = out + jnp.dot(p2.astype(jnp.bfloat16), v2, preferred_element_type=jnp.float32)
        out = (out / summed).reshape(TT, TH, cols, dim)
        for i in range(TT):
            for j in range(TH):
                f, row = t * TT + i, r * TH + j
                live = (flive[f] * rlive[row]) > 0
                o_ref[f, row] = jnp.where(live, out[i, j], 0.0).astype(o_ref.dtype)

    for near_t in range(2):
        for near_r in range(2):

            @pl.when((w0 == near_t) & (w1 == near_r))
            def _():
                for t in range(frames // TT):
                    for r in range(rows // TH):
                        tile(t, r, near_t, near_r)


def attend_call(qkv, ext, side, win, flive, rlive, kfe, kfy, qf, q_gain, k_gain):
    frames, rows, cols, channels = qkv.shape
    dim = q_gain.shape[0]
    heads = channels // (3 * dim)
    whole = lambda a: pl.BlockSpec(a.shape, lambda h, *_: (0,) * a.ndim)
    qg, kg = q_gain.reshape(1, dim), k_gain.reshape(1, dim)
    eb, yb = ext.shape[:3] + (dim,), side.shape[:2] + (dim,)
    grid_spec = pltpu.PrefetchScalarGridSpec(
        num_scalar_prefetch=3,
        grid=(heads,),
        in_specs=[
            pl.BlockSpec((frames, rows, cols, dim), lambda h, *_: (0, 0, 0, h)),
            pl.BlockSpec(eb, lambda h, *_: (0, 0, 0, h)),
            pl.BlockSpec(eb, lambda h, *_: (0, 0, 0, h + heads)),
            pl.BlockSpec(yb, lambda h, *_: (0, 0, h)),
            pl.BlockSpec(yb, lambda h, *_: (0, 0, h + heads)),
            whole(kfe),
            whole(kfy),
            whole(qf),
            whole(qg),
            whole(kg),
        ],
        out_specs=pl.BlockSpec((frames, rows, cols, dim), lambda h, *_: (0, 0, 0, h)),
        scratch_shapes=[
            pltpu.VMEM((frames, rows, cols, dim), jnp.bfloat16),
            pltpu.VMEM(eb, jnp.bfloat16),
            pltpu.VMEM(yb, jnp.bfloat16),
        ],
    )
    return pl.pallas_call(
        attend_kernel,
        grid_spec=grid_spec,
        out_shape=jax.ShapeDtypeStruct((frames, rows, cols, heads * dim), jnp.bfloat16),
        compiler_params=pltpu.CompilerParams(vmem_limit_bytes=40 * 1024 * 1024),
        cost_estimate=pl.CostEstimate(
            flops=4 * heads * frames * rows * cols * 1440 * dim,
            bytes_accessed=ext.size * 2 + side.size * 2 + qkv.size,
            transcendentals=heads * frames * rows * cols * 1440,
        ),
    )(win, flive, rlive, qkv, ext, ext, side, side, kfe, kfy, qf, qg, kg)


def shift(value, axis, step):
    size = lax.axis_size(axis)
    pairs = [(i, i + step) for i in range(size) if 0 <= i + step < size]
    return lax.ppermute(value, axis, pairs)


def tables(frames, rows, cols, windows, frame_counts, row_counts):
    swap = [(0, 1), (1, 0)]
    me = lax.axis_index("hd")
    other = lax.ppermute(windows, "hd", swap)
    win = jnp.where(me == 0, jnp.concatenate([windows, other]), jnp.concatenate([other, windows]))
    at_f = lax.axis_index("ta") * frames - TT + jnp.arange(frames + 2 * TT, dtype=jnp.int32)
    at_r = lax.axis_index("ha") * rows - TH + jnp.arange(rows + 2 * TH, dtype=jnp.int32)
    flive = valid_cells(at_f, TT, frame_counts)
    rlive = valid_cells(at_r, TH, row_counts)
    live = flive[:, None] & rlive[None, :]
    own = (me * cols + jnp.arange(cols, dtype=jnp.int32)) // TW
    beside = jnp.full((TW,), jnp.where(me == 0, cols // TW, cols // TW - 1), jnp.int32)
    lanes = jnp.arange(FEATURES, dtype=jnp.int32)

    def key_entries(tiles):
        hot = (tiles[:, None] == lanes[None, :])[None, None]
        dead = (~live)[:, :, None, None] & (lanes == FEATURES - 1)
        return jnp.where(hot | dead, 1.0, 0.0).astype(jnp.bfloat16)

    kfe = key_entries(own)
    kfy = key_entries(beside).reshape(frames + 2 * TT, (rows + 2 * TH) * TW, FEATURES)
    gap = jnp.abs(own[:, None] - lanes[None, :])
    far = jnp.stack([gap > 0, gap > 1]) | (lanes == FEATURES - 1)
    qf = jnp.where(far, MASKED, 0.0).astype(jnp.bfloat16)
    qf = jnp.broadcast_to(qf[:, None], (2, TT * TH, cols, FEATURES)).reshape(2, -1, FEATURES)
    count = lambda flags, width: flags.astype(jnp.int32)[width:-width]
    return win, count(flive, TT), count(rlive, TH), kfe, kfy, qf


def column_shards(qkv, q_gain, k_gain, windows, frame_counts, row_counts):
    frames, rows, cols, channels = qkv.shape
    kv = qkv[..., channels // 3 :]
    me = lax.axis_index("hd")
    edge = lax.dynamic_slice_in_dim(kv, jnp.where(me == 0, cols - TW, 0), TW, axis=2)
    side = lax.ppermute(edge, "hd", [(0, 1), (1, 0)])

    def grown(value):
        lo = shift(value[:, rows - TH :], "ha", 1)
        hi = shift(value[:, :TH], "ha", -1)
        value = jnp.concatenate([lo, value, hi], axis=1)
        lo = shift(value[frames - TT :], "ta", 1)
        hi = shift(value[:TT], "ta", -1)
        return jnp.concatenate([lo, value, hi], axis=0)

    ext = grown(kv)
    side = grown(side).reshape(frames + 2 * TT, -1, kv.shape[-1])
    made = tables(frames, rows, cols, windows, frame_counts, row_counts)
    return attend_call(qkv, ext, side, *made, q_gain, k_gain)


def solution(mesh):
    def shards(qkv, *rest):
        fits = mesh.shape["hd"] == 2 and qkv.shape[2] % 16 == 0
        return (column_shards if fits else head_shards)(qkv, *rest)

    return jax.shard_map(
        shards,
        mesh=mesh,
        in_specs=(P("ta", "ha", "hd", None), P(), P(), P("hd", None), P(), P()),
        out_specs=P("ta", "ha", "hd", None),
        check_vma=False,
    )
```

```python
import functools
import math

import jax
import jax.numpy as jnp
import numpy as np
from jax import lax
from jax.experimental import pallas as pl
from jax.experimental.pallas import tpu as pltpu
from jax.sharding import PartitionSpec as P

TT = 2
TH = 2
TW = 8


def extended(value, sides, width):
    for axis, dim in sides:
        size, length = (lax.axis_size(axis), value.shape[dim])
        up = [(i, (i + 1) % size) for i in range(size - 1)]
        down = [(j, i) for i, j in up]
        last = lax.slice_in_dim(value, length - width, length, axis=dim)
        initial = lax.slice_in_dim(value, 0, width, axis=dim)
        before = lax.ppermute(last, axis, up)
        after = lax.ppermute(initial, axis, down)
        value = jnp.concatenate([before, value, after], axis=dim)
    return value


def normalize(part_values, gain):
    widened = part_values.astype(jnp.float32)
    meansq = jnp.mean(widened * widened, axis=-1, keepdims=True)
    return (widened * lax.rsqrt(meansq + 1e-06) * gain).astype(jnp.bfloat16)


def valid_cells(position, extent, counts):
    tile_index = position // extent
    listed = jnp.arange(counts.shape[0], dtype=jnp.int32)
    holding = jnp.sum(jnp.where(tile_index[:, None] == listed[None, :], counts[None, :], 0), axis=1)
    return position % extent < holding


def extend_rims(paired):
    grown = extended(paired, (("ta", 0), ("ha", 1)), TT)
    return grown


def head_shards(qkv, q_gain, k_gain, windows, frame_counts, row_counts):
    frame_num, row_num, col_local, channels = qkv.shape
    head_dim = q_gain.shape[0]
    heads_all = channels // (3 * head_dim)
    sectioned = qkv.reshape(frame_num, row_num, col_local, 3, heads_all, head_dim)
    spread = lax.all_to_all(sectioned, "hd", split_axis=4, concat_axis=2, tiled=True)
    queries = normalize(spread[:, :, :, 0], q_gain)
    paired = jnp.stack([normalize(spread[:, :, :, 1], k_gain), spread[:, :, :, 2]], axis=3)
    padded = extend_rims(paired)
    col_num = queries.shape[2]
    heads_local = queries.shape[3]
    frame_base = lax.axis_index("ta") * frame_num
    row_base = lax.axis_index("ha") * row_num
    time_tiles = frame_num // TT
    score_scale = 1.0 / math.sqrt(head_dim)
    col_tiles = jnp.arange(col_num, dtype=jnp.int32) // TW
    col_gap = jnp.abs(col_tiles[:, None] - col_tiles[None, :])
    query_rows = row_base + jnp.arange(row_num, dtype=jnp.int32)
    key_rows = row_base - TH + jnp.arange(row_num + 2 * TH, dtype=jnp.int32)
    row_gap = jnp.abs(query_rows[:, None] // TH - key_rows[None, :] // TH)
    row_valid = valid_cells(key_rows, TH, row_counts)
    query_row_valid = valid_cells(query_rows, TH, row_counts)

    def attend(item_index):
        tile_at = item_index // heads_local
        head_at = item_index % heads_local
        first_frame = tile_at * TT
        query_block = lax.dynamic_slice(
            queries, (first_frame, 0, 0, head_at, 0), (TT, row_num, col_num, 1, head_dim)
        ).reshape(-1, head_dim)
        pair_block = lax.dynamic_slice(
            padded,
            (first_frame, 0, 0, 0, head_at, 0),
            (3 * TT, row_num + 2 * TH, col_num, 2, 1, head_dim),
        )
        key_block = pair_block[:, :, :, 0, 0].reshape(-1, head_dim)
        value_block = pair_block[:, :, :, 1, 0].reshape(-1, head_dim)
        radius = windows[head_at]
        query_frames = frame_base + first_frame + jnp.arange(TT, dtype=jnp.int32)
        key_frames = frame_base + first_frame - TT + jnp.arange(3 * TT, dtype=jnp.int32)
        time_mask = (
            jnp.abs(query_frames[:, None] // TT - key_frames[None, :] // TT) <= radius[0]
        ) & valid_cells(key_frames, TT, frame_counts)[None, :]
        row_mask = (row_gap <= radius[1]) & row_valid[None, :]
        col_mask = col_gap <= radius[2]
        allowed = (
            time_mask[:, None, None, :, None, None]
            & row_mask[None, :, None, None, :, None]
            & col_mask[None, None, :, None, None, :]
        ).reshape(query_block.shape[0], key_block.shape[0])
        query_live = (
            valid_cells(query_frames, TT, frame_counts)[:, None, None]
            & query_row_valid[None, :, None]
            & (col_tiles >= 0)[None, None, :]
        ).reshape(-1)
        scores = (
            jnp.einsum("qd,kd->qk", query_block, key_block, preferred_element_type=jnp.float32)
            * score_scale
        )
        scores = jnp.where(allowed, scores, -1e30)
        highest = jnp.max(scores, axis=1, keepdims=True)
        raised = jnp.exp(scores - highest)
        summed = jnp.sum(raised, axis=1, keepdims=True)
        weights = raised.astype(jnp.bfloat16)
        blended = jnp.dot(weights, value_block, preferred_element_type=jnp.float32)
        result = jnp.where(query_live[:, None], blended / summed, 0.0)
        return result.astype(jnp.bfloat16).reshape(TT, row_num, col_num, head_dim)

    outputs = lax.map(attend, jnp.arange(time_tiles * heads_local, dtype=jnp.int32))
    outputs = outputs.reshape(time_tiles, heads_local, TT, row_num, col_num, head_dim)
    outputs = outputs.transpose(0, 2, 3, 4, 1, 5).reshape(
        frame_num, row_num, col_num, heads_local, head_dim
    )
    gathered = lax.all_to_all(outputs, "hd", split_axis=2, concat_axis=3, tiled=True)
    return gathered.reshape(frame_num, row_num, col_local, heads_all * head_dim)


MASKED = -1e30
FEATURES = 128


def unit_rms(raw, gain):
    wide = raw.astype(jnp.float32)
    meansq = jnp.mean(wide * wide, axis=-1, keepdims=True)
    return (wide * lax.rsqrt(meansq + 1e-06) * gain).astype(jnp.bfloat16)


def attend_kernel(
    win, flive, rlive, q_ref, ke_ref, ve_ref, ky_ref, vy_ref, kfe_ref, kfy_ref, qf_ref,
    qg_ref, kg_ref, o_ref, qn, kn, kyn,
):
    frames, rows, cols, dim = q_ref.shape
    halo = ky_ref.shape[1] // (rows + 2 * TH)
    head = pl.program_id(0)
    w0, w1, w2 = win[head, 0], win[head, 1], win[head, 2]
    qg, kg = qg_ref[...], kg_ref[...]
    for f in range(frames):
        qn[f] = unit_rms(q_ref[f], qg)
    for f in range(frames + 2 * TT):
        kn[f] = unit_rms(ke_ref[f], kg)
        kyn[f] = unit_rms(ky_ref[f], kg)
    factor = math.log2(math.e) / math.sqrt(dim)

    def tile(t, r, near_t, near_r):
        fs = slice(t * TT + TT * (1 - near_t), t * TT + TT * (2 + near_t))
        r0, r1 = r * TH + TH * (1 - near_r), r * TH + TH * (2 + near_r)
        rs, ys = slice(r0, r1), slice(r0 * halo, r1 * halo)
        q = qn[t * TT : (t + 1) * TT, r * TH : (r + 1) * TH].reshape(-1, dim)
        q = jnp.concatenate([q, qf_ref[w2]], axis=1)
        nt = (((1,), (1,)), ((), ()))
        k1 = jnp.concatenate([kn[fs, rs].reshape(-1, dim), kfe_ref[fs, rs].reshape(-1, FEATURES)], axis=1)
        k2 = jnp.concatenate([kyn[fs, ys].reshape(-1, dim), kfy_ref[fs, ys].reshape(-1, FEATURES)], axis=1)
        s1 = lax.dot_general(q, k1, nt, preferred_element_type=jnp.float32)
        s2 = lax.dot_general(q, k2, nt, preferred_element_type=jnp.float32)
        top = jnp.maximum(jnp.max(s1, axis=1, keepdims=True), jnp.max(s2, axis=1, keepdims=True))
        p1 = jnp.exp2((s1 - top) * factor)
        p2 = jnp.exp2((s2 - top) * factor)
        summed = jnp.sum(p1, axis=1, keepdims=True) + jnp.sum(p2, axis=1, keepdims=True)
        v1 = ve_ref[fs, rs].reshape(-1, dim)
        v2 = vy_ref[fs, ys].reshape(-1, dim)
        out = jnp.dot(p1.astype(jnp.bfloat16), v1, preferred_element_type=jnp.float32)
        out = out + jnp.dot(p2.astype(jnp.bfloat16), v2, preferred_element_type=jnp.float32)
        out = (out / summed).reshape(TT, TH, cols, dim)
        for i in range(TT):
            for j in range(TH):
                f, row = t * TT + i, r * TH + j
                live = (flive[f] * rlive[row]) > 0
                o_ref[f, row] = jnp.where(live, out[i, j], 0.0).astype(o_ref.dtype)

    for near_t in range(2):
        for near_r in range(2):

            @pl.when((w0 == near_t) & (w1 == near_r))
            def _():
                for t in range(frames // TT):
                    for r in range(rows // TH):
                        tile(t, r, near_t, near_r)


def attend_call(qkv, ext, side, win, flive, rlive, kfe, kfy, qf, q_gain, k_gain):
    frames, rows, cols, channels = qkv.shape
    dim = q_gain.shape[0]
    heads = channels // (3 * dim)
    whole = lambda a: pl.BlockSpec(a.shape, lambda h, *_: (0,) * a.ndim)
    qg, kg = q_gain.reshape(1, dim), k_gain.reshape(1, dim)
    eb, yb = ext.shape[:3] + (dim,), side.shape[:2] + (dim,)
    grid_spec = pltpu.PrefetchScalarGridSpec(
        num_scalar_prefetch=3,
        grid=(heads,),
        in_specs=[
            pl.BlockSpec((frames, rows, cols, dim), lambda h, *_: (0, 0, 0, h)),
            pl.BlockSpec(eb, lambda h, *_: (0, 0, 0, h)),
            pl.BlockSpec(eb, lambda h, *_: (0, 0, 0, h + heads)),
            pl.BlockSpec(yb, lambda h, *_: (0, 0, h)),
            pl.BlockSpec(yb, lambda h, *_: (0, 0, h + heads)),
            whole(kfe),
            whole(kfy),
            whole(qf),
            whole(qg),
            whole(kg),
        ],
        out_specs=pl.BlockSpec((frames, rows, cols, dim), lambda h, *_: (0, 0, 0, h)),
        scratch_shapes=[
            pltpu.VMEM((frames, rows, cols, dim), jnp.bfloat16),
            pltpu.VMEM(eb, jnp.bfloat16),
            pltpu.VMEM(yb, jnp.bfloat16),
        ],
    )
    return pl.pallas_call(
        attend_kernel,
        grid_spec=grid_spec,
        out_shape=jax.ShapeDtypeStruct((frames, rows, cols, heads * dim), jnp.bfloat16),
        compiler_params=pltpu.CompilerParams(vmem_limit_bytes=40 * 1024 * 1024),
        cost_estimate=pl.CostEstimate(
            flops=4 * heads * frames * rows * cols * 1440 * dim,
            bytes_accessed=ext.size * 2 + side.size * 2 + qkv.size,
            transcendentals=heads * frames * rows * cols * 1440,
        ),
    )(win, flive, rlive, qkv, ext, ext, side, side, kfe, kfy, qf, qg, kg)


def shift(value, axis, step):
    size = lax.axis_size(axis)
    pairs = [(i, i + step) for i in range(size) if 0 <= i + step < size]
    return lax.ppermute(value, axis, pairs)


def tables(frames, rows, cols, windows, frame_counts, row_counts):
    swap = [(0, 1), (1, 0)]
    me = lax.axis_index("hd")
    other = lax.ppermute(windows, "hd", swap)
    win = jnp.where(me == 0, jnp.concatenate([windows, other]), jnp.concatenate([other, windows]))
    at_f = lax.axis_index("ta") * frames - TT + jnp.arange(frames + 2 * TT, dtype=jnp.int32)
    at_r = lax.axis_index("ha") * rows - TH + jnp.arange(rows + 2 * TH, dtype=jnp.int32)
    flive = valid_cells(at_f, TT, frame_counts)
    rlive = valid_cells(at_r, TH, row_counts)
    live = flive[:, None] & rlive[None, :]
    own = (me * cols + jnp.arange(cols, dtype=jnp.int32)) // TW
    beside = jnp.full((TW,), jnp.where(me == 0, cols // TW, cols // TW - 1), jnp.int32)
    lanes = jnp.arange(FEATURES, dtype=jnp.int32)

    def key_entries(tiles):
        hot = (tiles[:, None] == lanes[None, :])[None, None]
        dead = (~live)[:, :, None, None] & (lanes == FEATURES - 1)
        return jnp.where(hot | dead, 1.0, 0.0).astype(jnp.bfloat16)

    kfe = key_entries(own)
    kfy = key_entries(beside).reshape(frames + 2 * TT, (rows + 2 * TH) * TW, FEATURES)
    gap = jnp.abs(own[:, None] - lanes[None, :])
    far = jnp.stack([gap > 0, gap > 1]) | (lanes == FEATURES - 1)
    qf = jnp.where(far, MASKED, 0.0).astype(jnp.bfloat16)
    qf = jnp.broadcast_to(qf[:, None], (2, TT * TH, cols, FEATURES)).reshape(2, -1, FEATURES)
    count = lambda flags, width: flags.astype(jnp.int32)[width:-width]
    return win, count(flive, TT), count(rlive, TH), kfe, kfy, qf


CHUNKS = 6
MESH = pl.DeviceIdType.MESH
Y_OWN, Z_UP, Z_DOWN, ZS_UP, ZS_DOWN, X_UP, X_DOWN, XLO_UP, XLO_DOWN, XHI_UP, XHI_DOWN, XS_UP, XS_DOWN = range(13)
KINDS = 13


def halo_kernel(sizes, base, qkv, edge, ext, side, send_sem, recv_sem, own_sem):
    frames, rows = qkv.shape[:2]
    f1, r1 = frames + TT, rows + TH
    width = ext.shape[-1] // CHUNKS
    at = {axis: lax.axis_index(axis) for axis in sizes}
    up = {axis: at[axis] < sizes[axis] - 1 for axis in ("ta", "ha")}
    down = {axis: at[axis] > 0 for axis in ("ta", "ha")}
    partner = {"hd": 1 - at["hd"]}

    barrier = pltpu.get_barrier_semaphore()
    pl.semaphore_signal(barrier, inc=1, device_id=partner, device_id_type=MESH)
    for axis in ("ta", "ha"):
        for there, step in ((up[axis], 1), (down[axis], -1)):

            @pl.when(there)
            def _():
                pl.semaphore_signal(barrier, inc=1, device_id={axis: at[axis] + step}, device_id_type=MESH)

    greeted = 1
    for axis in ("ta", "ha"):
        greeted = greeted + up[axis].astype(jnp.int32) + down[axis].astype(jnp.int32)
    pl.semaphore_wait(barrier, greeted)

    def lanes(c):
        return pl.ds(c * width, width)

    def own(fs, rs, c):
        return qkv.at[fs, rs, :, pl.ds(base + c * width, width)]

    def cells(fs, rs, c):
        return ext.at[fs, rs, :, lanes(c)]

    def strip(fs, rs, c, ref=side):
        return ref.at[fs, slice(rs.start * TW, rs.stop * TW), lanes(c)]

    def remote(kind, c, src, dst, device):
        return pltpu.make_async_remote_copy(
            src_ref=src, dst_ref=dst, send_sem=send_sem.at[kind, c], recv_sem=recv_sem.at[kind, c],
            device_id=device, device_id_type=MESH,
        )

    F, R = slice(TT, f1), slice(TH, r1)
    LO, HI = slice(0, TT), slice(f1, f1 + TT)
    RLO, RHI = slice(0, TH), slice(r1, r1 + TH)
    OF = slice(0, frames)
    first, last = slice(0, TT), slice(frames - TT, frames)
    rfirst, rlast = slice(0, TH), slice(rows - TH, rows)
    flast, ffirst = slice(frames, f1), slice(TT, 2 * TT)
    ROWS_ALL = slice(0, rows + 2 * TH)

    def plan(kind, c):
        return {
            Z_UP: ("ha", 1, own(OF, rlast, c), cells(F, RLO, c), own(OF, rfirst, c)),
            Z_DOWN: ("ha", -1, own(OF, rfirst, c), cells(F, RHI, c), own(OF, rfirst, c)),
            ZS_UP: ("ha", 1, strip(F, slice(rows, r1), c), strip(F, RLO, c), strip(OF, rfirst, c, edge)),
            ZS_DOWN: ("ha", -1, strip(F, slice(TH, 2 * TH), c), strip(F, RHI, c), strip(OF, rfirst, c, edge)),
            X_UP: ("ta", 1, own(last, slice(0, rows), c), cells(LO, R, c), own(first, slice(0, rows), c)),
            X_DOWN: ("ta", -1, own(first, slice(0, rows), c), cells(HI, R, c), own(first, slice(0, rows), c)),
            XLO_UP: ("ta", 1, cells(flast, RLO, c), cells(LO, RLO, c), own(first, rfirst, c)),
            XLO_DOWN: ("ta", -1, cells(ffirst, RLO, c), cells(HI, RLO, c), own(first, rfirst, c)),
            XHI_UP: ("ta", 1, cells(flast, RHI, c), cells(LO, RHI, c), own(first, rfirst, c)),
            XHI_DOWN: ("ta", -1, cells(ffirst, RHI, c), cells(HI, RHI, c), own(first, rfirst, c)),
            XS_UP: ("ta", 1, strip(flast, ROWS_ALL, c), strip(LO, ROWS_ALL, c), None),
            XS_DOWN: ("ta", -1, strip(ffirst, ROWS_ALL, c), strip(HI, ROWS_ALL, c), None),
        }[kind]

    def start(kind, c):
        axis, step, src, dst, fill = plan(kind, c)
        if fill is None:
            fill = strip(ffirst, ROWS_ALL, c)
        sends, gets = (up, down) if step == 1 else (down, up)

        @pl.when(sends[axis])
        def _():
            remote(kind, c, src, dst, {axis: at[axis] + step}).start()

        @pl.when(jnp.logical_not(gets[axis]))
        def _():
            pltpu.make_async_copy(fill, dst, recv_sem.at[kind, c]).start()

    def got(kind, c):
        dst = plan(kind, c)[3]
        pltpu.make_async_copy(dst, dst, recv_sem.at[kind, c]).wait()

    def sent(kind, c):
        axis, step, src, dst, _ = plan(kind, c)

        @pl.when((up if step == 1 else down)[axis])
        def _():
            remote(kind, c, src, dst, {axis: at[axis] + step}).wait_send()

    def y_copy(c):
        return remote(Y_OWN, c, strip(OF, slice(0, rows), c, edge), strip(F, R, c), partner)

    def home(c):
        return pltpu.make_async_copy(own(OF, slice(0, rows), c), cells(F, R, c), own_sem.at[c])

    ahead = 2
    for c in range(CHUNKS):
        y_copy(c).start()
    for c in range(CHUNKS + ahead):
        if c < CHUNKS:
            for kind in (Z_UP, Z_DOWN, X_UP, X_DOWN):
                start(kind, c)
            home(c).start()
        d = c - 1
        if 0 <= d < CHUNKS:
            y_copy(d).wait_recv()
            start(ZS_UP, d)
            start(ZS_DOWN, d)
        e = c - ahead
        if 0 <= e < CHUNKS:
            got(Z_UP, e)
            start(XLO_UP, e)
            start(XLO_DOWN, e)
            got(Z_DOWN, e)
            start(XHI_UP, e)
            start(XHI_DOWN, e)
            got(ZS_UP, e)
            got(ZS_DOWN, e)
            start(XS_UP, e)
            start(XS_DOWN, e)
    for c in range(CHUNKS):
        home(c).wait()
        y_copy(c).wait_send()
        for kind in range(Z_UP, KINDS):
            sent(kind, c)
            if kind >= X_UP:
                got(kind, c)


def halo_call(mesh, qkv, edge):
    frames, rows, cols, channels = qkv.shape
    wide = edge.shape[-1]
    sizes = {axis: mesh.shape[axis] for axis in ("ta", "ha", "hd")}
    hbm = pl.BlockSpec(memory_space=pl.ANY)
    return pl.pallas_call(
        functools.partial(halo_kernel, sizes, channels - wide),
        in_specs=[hbm, hbm],
        out_specs=[hbm, hbm],
        out_shape=[
            jax.ShapeDtypeStruct((frames + 2 * TT, rows + 2 * TH, cols, wide), qkv.dtype),
            jax.ShapeDtypeStruct((frames + 2 * TT, (rows + 2 * TH) * TW, wide), qkv.dtype),
        ],
        scratch_shapes=[
            pltpu.SemaphoreType.DMA((KINDS, CHUNKS)),
            pltpu.SemaphoreType.DMA((KINDS, CHUNKS)),
            pltpu.SemaphoreType.DMA((CHUNKS,)),
        ],
        compiler_params=pltpu.CompilerParams(collective_id=0, has_side_effects=True),
    )(qkv, edge)


def column_shards(mesh, qkv, q_gain, k_gain, windows, frame_counts, row_counts):
    frames, rows, cols, channels = qkv.shape
    wide = channels // 3 * 2
    me = lax.axis_index("hd")
    zero = jnp.zeros((), jnp.int32)
    edge = lax.dynamic_slice(
        qkv, (zero, zero, jnp.where(me == 0, cols - TW, 0), zero + channels - wide), (frames, rows, TW, wide)
    ).reshape(frames, rows * TW, wide)
    ext, side = halo_call(mesh, qkv, edge)
    made = tables(frames, rows, cols, windows, frame_counts, row_counts)
    return attend_call(qkv, ext, side, *made, q_gain, k_gain)


def solution(mesh):
    def shards(qkv, *rest):
        fits = mesh.shape["hd"] == 2 and min(mesh.shape["ta"], mesh.shape["ha"]) > 1 and qkv.shape[2] % 16 == 0
        return column_shards(mesh, qkv, *rest) if fits else head_shards(qkv, *rest)

    return jax.shard_map(
        shards,
        mesh=mesh,
        in_specs=(P("ta", "ha", "hd", None), P(), P(), P("hd", None), P(), P()),
        out_specs=P("ta", "ha", "hd", None),
        check_vma=False,
    )
```

```python
import functools
import math

import jax
import jax.numpy as jnp
import numpy as np
from jax import lax
from jax.experimental import pallas as pl
from jax.experimental.pallas import tpu as pltpu
from jax.sharding import PartitionSpec as P

TT = 2
TH = 2
TW = 8


def extended(value, sides, width):
    for axis, dim in sides:
        size, length = (lax.axis_size(axis), value.shape[dim])
        up = [(i, (i + 1) % size) for i in range(size - 1)]
        down = [(j, i) for i, j in up]
        last = lax.slice_in_dim(value, length - width, length, axis=dim)
        initial = lax.slice_in_dim(value, 0, width, axis=dim)
        before = lax.ppermute(last, axis, up)
        after = lax.ppermute(initial, axis, down)
        value = jnp.concatenate([before, value, after], axis=dim)
    return value


def normalize(part_values, gain):
    widened = part_values.astype(jnp.float32)
    meansq = jnp.mean(widened * widened, axis=-1, keepdims=True)
    return (widened * lax.rsqrt(meansq + 1e-06) * gain).astype(jnp.bfloat16)


def valid_cells(position, extent, counts):
    tile_index = position // extent
    listed = jnp.arange(counts.shape[0], dtype=jnp.int32)
    holding = jnp.sum(jnp.where(tile_index[:, None] == listed[None, :], counts[None, :], 0), axis=1)
    return position % extent < holding


def extend_rims(paired):
    grown = extended(paired, (("ta", 0), ("ha", 1)), TT)
    return grown


def head_shards(qkv, q_gain, k_gain, windows, frame_counts, row_counts):
    frame_num, row_num, col_local, channels = qkv.shape
    head_dim = q_gain.shape[0]
    heads_all = channels // (3 * head_dim)
    sectioned = qkv.reshape(frame_num, row_num, col_local, 3, heads_all, head_dim)
    spread = lax.all_to_all(sectioned, "hd", split_axis=4, concat_axis=2, tiled=True)
    queries = normalize(spread[:, :, :, 0], q_gain)
    paired = jnp.stack([normalize(spread[:, :, :, 1], k_gain), spread[:, :, :, 2]], axis=3)
    padded = extend_rims(paired)
    col_num = queries.shape[2]
    heads_local = queries.shape[3]
    frame_base = lax.axis_index("ta") * frame_num
    row_base = lax.axis_index("ha") * row_num
    time_tiles = frame_num // TT
    score_scale = 1.0 / math.sqrt(head_dim)
    col_tiles = jnp.arange(col_num, dtype=jnp.int32) // TW
    col_gap = jnp.abs(col_tiles[:, None] - col_tiles[None, :])
    query_rows = row_base + jnp.arange(row_num, dtype=jnp.int32)
    key_rows = row_base - TH + jnp.arange(row_num + 2 * TH, dtype=jnp.int32)
    row_gap = jnp.abs(query_rows[:, None] // TH - key_rows[None, :] // TH)
    row_valid = valid_cells(key_rows, TH, row_counts)
    query_row_valid = valid_cells(query_rows, TH, row_counts)

    def attend(item_index):
        tile_at = item_index // heads_local
        head_at = item_index % heads_local
        first_frame = tile_at * TT
        query_block = lax.dynamic_slice(
            queries, (first_frame, 0, 0, head_at, 0), (TT, row_num, col_num, 1, head_dim)
        ).reshape(-1, head_dim)
        pair_block = lax.dynamic_slice(
            padded,
            (first_frame, 0, 0, 0, head_at, 0),
            (3 * TT, row_num + 2 * TH, col_num, 2, 1, head_dim),
        )
        key_block = pair_block[:, :, :, 0, 0].reshape(-1, head_dim)
        value_block = pair_block[:, :, :, 1, 0].reshape(-1, head_dim)
        radius = windows[head_at]
        query_frames = frame_base + first_frame + jnp.arange(TT, dtype=jnp.int32)
        key_frames = frame_base + first_frame - TT + jnp.arange(3 * TT, dtype=jnp.int32)
        time_mask = (
            jnp.abs(query_frames[:, None] // TT - key_frames[None, :] // TT) <= radius[0]
        ) & valid_cells(key_frames, TT, frame_counts)[None, :]
        row_mask = (row_gap <= radius[1]) & row_valid[None, :]
        col_mask = col_gap <= radius[2]
        allowed = (
            time_mask[:, None, None, :, None, None]
            & row_mask[None, :, None, None, :, None]
            & col_mask[None, None, :, None, None, :]
        ).reshape(query_block.shape[0], key_block.shape[0])
        query_live = (
            valid_cells(query_frames, TT, frame_counts)[:, None, None]
            & query_row_valid[None, :, None]
            & (col_tiles >= 0)[None, None, :]
        ).reshape(-1)
        scores = (
            jnp.einsum("qd,kd->qk", query_block, key_block, preferred_element_type=jnp.float32)
            * score_scale
        )
        scores = jnp.where(allowed, scores, -1e30)
        highest = jnp.max(scores, axis=1, keepdims=True)
        raised = jnp.exp(scores - highest)
        summed = jnp.sum(raised, axis=1, keepdims=True)
        weights = raised.astype(jnp.bfloat16)
        blended = jnp.dot(weights, value_block, preferred_element_type=jnp.float32)
        result = jnp.where(query_live[:, None], blended / summed, 0.0)
        return result.astype(jnp.bfloat16).reshape(TT, row_num, col_num, head_dim)

    outputs = lax.map(attend, jnp.arange(time_tiles * heads_local, dtype=jnp.int32))
    outputs = outputs.reshape(time_tiles, heads_local, TT, row_num, col_num, head_dim)
    outputs = outputs.transpose(0, 2, 3, 4, 1, 5).reshape(
        frame_num, row_num, col_num, heads_local, head_dim
    )
    gathered = lax.all_to_all(outputs, "hd", split_axis=2, concat_axis=3, tiled=True)
    return gathered.reshape(frame_num, row_num, col_local, heads_all * head_dim)


MASKED = -1e30
FEATURES = 128


def unit_rms(raw, gain):
    wide = raw.astype(jnp.float32)
    meansq = jnp.mean(wide * wide, axis=-1, keepdims=True)
    return (wide * lax.rsqrt(meansq + 1e-06) * gain).astype(jnp.bfloat16)


def attend_kernel(
    win, flive, rlive, fin, rin, q_ref, k_ref, v_ref, ke_ref, ve_ref, ky_ref, vy_ref, kfe_ref, kfy_ref,
    qf_ref, qg_ref, kg_ref, o_ref, qn, kn, kyn, vn, vyn,
):
    frames, rows, cols, dim = q_ref.shape
    halo = ky_ref.shape[1] // (rows + 2 * TH)
    head = pl.program_id(0)
    w0, w1, w2 = win[head, 0], win[head, 1], win[head, 2]
    qg, kg = qg_ref[...], kg_ref[...]
    for f in range(frames):
        qn[f] = unit_rms(q_ref[f], qg)
    for f in range(frames + 2 * TT):
        for r0, r1 in ((0, TH), (TH, TH + rows), (TH + rows, rows + 2 * TH)):
            held = (fin[f] * rin[r0]) > 0
            rs, ys = slice(r0, r1), slice(r0 * halo, r1 * halo)
            there = lambda x: lax.select(held, x, jnp.zeros_like(x))
            kyn[f, ys] = unit_rms(there(ky_ref[f, ys]), kg)
            vyn[f, ys] = there(vy_ref[f, ys])
            if TT <= f < frames + TT and r0 == TH:
                kn[f, rs] = unit_rms(k_ref[f - TT], kg)
                vn[f, rs] = v_ref[f - TT]
            else:
                kn[f, rs] = unit_rms(there(ke_ref[f, rs]), kg)
                vn[f, rs] = there(ve_ref[f, rs])
    factor = math.log2(math.e) / math.sqrt(dim)

    def tile(t, r, near_t, near_r):
        fs = slice(t * TT + TT * (1 - near_t), t * TT + TT * (2 + near_t))
        r0, r1 = r * TH + TH * (1 - near_r), r * TH + TH * (2 + near_r)
        rs, ys = slice(r0, r1), slice(r0 * halo, r1 * halo)
        q = qn[t * TT : (t + 1) * TT, r * TH : (r + 1) * TH].reshape(-1, dim)
        q = jnp.concatenate([q, qf_ref[w2]], axis=1)
        nt = (((1,), (1,)), ((), ()))
        k1 = jnp.concatenate([kn[fs, rs].reshape(-1, dim), kfe_ref[fs, rs].reshape(-1, FEATURES)], axis=1)
        k2 = jnp.concatenate([kyn[fs, ys].reshape(-1, dim), kfy_ref[fs, ys].reshape(-1, FEATURES)], axis=1)
        s1 = lax.dot_general(q, k1, nt, preferred_element_type=jnp.float32)
        s2 = lax.dot_general(q, k2, nt, preferred_element_type=jnp.float32)
        top = jnp.maximum(jnp.max(s1, axis=1, keepdims=True), jnp.max(s2, axis=1, keepdims=True))
        p1 = jnp.exp2((s1 - top) * factor)
        p2 = jnp.exp2((s2 - top) * factor)
        summed = jnp.sum(p1, axis=1, keepdims=True) + jnp.sum(p2, axis=1, keepdims=True)
        v1 = vn[fs, rs].reshape(-1, dim)
        v2 = vyn[fs, ys].reshape(-1, dim)
        out = jnp.dot(p1.astype(jnp.bfloat16), v1, preferred_element_type=jnp.float32)
        out = out + jnp.dot(p2.astype(jnp.bfloat16), v2, preferred_element_type=jnp.float32)
        out = (out / summed).reshape(TT, TH, cols, dim)
        for i in range(TT):
            for j in range(TH):
                f, row = t * TT + i, r * TH + j
                live = (flive[f] * rlive[row]) > 0
                o_ref[f, row] = jnp.where(live, out[i, j], 0.0).astype(o_ref.dtype)

    for near_t in range(2):
        for near_r in range(2):

            @pl.when((w0 == near_t) & (w1 == near_r))
            def _():
                for t in range(frames // TT):
                    for r in range(rows // TH):
                        tile(t, r, near_t, near_r)


def attend_call(qkv, ext, side, win, flive, rlive, fin, rin, kfe, kfy, qf, q_gain, k_gain):
    frames, rows, cols, channels = qkv.shape
    dim = q_gain.shape[0]
    heads = channels // (3 * dim)
    whole = lambda a: pl.BlockSpec(a.shape, lambda h, *_: (0,) * a.ndim)
    qg, kg = q_gain.reshape(1, dim), k_gain.reshape(1, dim)
    eb, yb = ext.shape[:3] + (dim,), side.shape[:2] + (dim,)
    grid_spec = pltpu.PrefetchScalarGridSpec(
        num_scalar_prefetch=5,
        grid=(heads,),
        in_specs=[
            pl.BlockSpec((frames, rows, cols, dim), lambda h, *_: (0, 0, 0, h)),
            pl.BlockSpec((frames, rows, cols, dim), lambda h, *_: (0, 0, 0, h + heads)),
            pl.BlockSpec((frames, rows, cols, dim), lambda h, *_: (0, 0, 0, h + 2 * heads)),
            pl.BlockSpec(eb, lambda h, *_: (0, 0, 0, h)),
            pl.BlockSpec(eb, lambda h, *_: (0, 0, 0, h + heads)),
            pl.BlockSpec(yb, lambda h, *_: (0, 0, h)),
            pl.BlockSpec(yb, lambda h, *_: (0, 0, h + heads)),
            whole(kfe),
            whole(kfy),
            whole(qf),
            whole(qg),
            whole(kg),
        ],
        out_specs=pl.BlockSpec((frames, rows, cols, dim), lambda h, *_: (0, 0, 0, h)),
        scratch_shapes=[
            pltpu.VMEM((frames, rows, cols, dim), jnp.bfloat16),
            pltpu.VMEM(eb, jnp.bfloat16),
            pltpu.VMEM(yb, jnp.bfloat16),
            pltpu.VMEM(eb, jnp.bfloat16),
            pltpu.VMEM(yb, jnp.bfloat16),
        ],
    )
    return pl.pallas_call(
        attend_kernel,
        grid_spec=grid_spec,
        out_shape=jax.ShapeDtypeStruct((frames, rows, cols, heads * dim), jnp.bfloat16),
        compiler_params=pltpu.CompilerParams(vmem_limit_bytes=40 * 1024 * 1024),
        cost_estimate=pl.CostEstimate(
            flops=4 * heads * frames * rows * cols * 1440 * dim,
            bytes_accessed=ext.size * 2 + side.size * 2 + qkv.size,
            transcendentals=heads * frames * rows * cols * 1440,
        ),
    )(win, flive, rlive, fin, rin, qkv, qkv, qkv, ext, ext, side, side, kfe, kfy, qf, qg, kg)


def shift(value, axis, step):
    size = lax.axis_size(axis)
    pairs = [(i, i + step) for i in range(size) if 0 <= i + step < size]
    return lax.ppermute(value, axis, pairs)


def tables(frames, rows, cols, windows, frame_counts, row_counts):
    swap = [(0, 1), (1, 0)]
    me = lax.axis_index("hd")
    other = lax.ppermute(windows, "hd", swap)
    win = jnp.where(me == 0, jnp.concatenate([windows, other]), jnp.concatenate([other, windows]))
    at_f = lax.axis_index("ta") * frames - TT + jnp.arange(frames + 2 * TT, dtype=jnp.int32)
    at_r = lax.axis_index("ha") * rows - TH + jnp.arange(rows + 2 * TH, dtype=jnp.int32)
    flive = valid_cells(at_f, TT, frame_counts)
    rlive = valid_cells(at_r, TH, row_counts)
    live = flive[:, None] & rlive[None, :]
    own = (me * cols + jnp.arange(cols, dtype=jnp.int32)) // TW
    beside = jnp.full((TW,), jnp.where(me == 0, cols // TW, cols // TW - 1), jnp.int32)
    lanes = jnp.arange(FEATURES, dtype=jnp.int32)

    def key_entries(tiles):
        hot = (tiles[:, None] == lanes[None, :])[None, None]
        dead = (~live)[:, :, None, None] & (lanes == FEATURES - 1)
        return jnp.where(hot | dead, 1.0, 0.0).astype(jnp.bfloat16)

    kfe = key_entries(own)
    kfy = key_entries(beside).reshape(frames + 2 * TT, (rows + 2 * TH) * TW, FEATURES)
    gap = jnp.abs(own[:, None] - lanes[None, :])
    far = jnp.stack([gap > 0, gap > 1]) | (lanes == FEATURES - 1)
    qf = jnp.where(far, MASKED, 0.0).astype(jnp.bfloat16)
    qf = jnp.broadcast_to(qf[:, None], (2, TT * TH, cols, FEATURES)).reshape(2, -1, FEATURES)
    count = lambda flags, width: flags.astype(jnp.int32)[width:-width]
    inside = lambda at, counts, extent: ((at >= 0) & (at < counts.shape[0] * extent)).astype(jnp.int32)
    fin, rin = inside(at_f, frame_counts, TT), inside(at_r, row_counts, TH)
    return win, count(flive, TT), count(rlive, TH), fin, rin, kfe, kfy, qf


CHUNKS = 6
MESH = pl.DeviceIdType.MESH
Y_OWN, Z_UP, Z_DOWN, ZS_UP, ZS_DOWN, X_UP, X_DOWN, XLO_UP, XLO_DOWN, XHI_UP, XHI_DOWN, XS_UP, XS_DOWN = range(13)
KINDS = 13


def halo_kernel(sizes, base, qkv, edge, ext, side, send_sem, recv_sem):
    frames, rows = qkv.shape[:2]
    f1, r1 = frames + TT, rows + TH
    width = ext.shape[-1] // CHUNKS
    at = {axis: lax.axis_index(axis) for axis in sizes}
    up = {axis: at[axis] < sizes[axis] - 1 for axis in ("ta", "ha")}
    down = {axis: at[axis] > 0 for axis in ("ta", "ha")}
    partner = {"hd": 1 - at["hd"]}

    barrier = pltpu.get_barrier_semaphore()
    pl.semaphore_signal(barrier, inc=1, device_id=partner, device_id_type=MESH)
    for axis in ("ta", "ha"):
        for there, step in ((up[axis], 1), (down[axis], -1)):

            @pl.when(there)
            def _():
                pl.semaphore_signal(barrier, inc=1, device_id={axis: at[axis] + step}, device_id_type=MESH)

    greeted = 1
    for axis in ("ta", "ha"):
        greeted = greeted + up[axis].astype(jnp.int32) + down[axis].astype(jnp.int32)
    pl.semaphore_wait(barrier, greeted)

    def lanes(c):
        return pl.ds(c * width, width)

    def own(fs, rs, c):
        return qkv.at[fs, rs, :, pl.ds(base + c * width, width)]

    def cells(fs, rs, c):
        return ext.at[fs, rs, :, lanes(c)]

    def strip(fs, rs, c, ref=side):
        return ref.at[fs, slice(rs.start * TW, rs.stop * TW), lanes(c)]

    def remote(kind, c, src, dst, device):
        return pltpu.make_async_remote_copy(
            src_ref=src, dst_ref=dst, send_sem=send_sem.at[kind, c], recv_sem=recv_sem.at[kind, c],
            device_id=device, device_id_type=MESH,
        )

    F, R = slice(TT, f1), slice(TH, r1)
    LO, HI = slice(0, TT), slice(f1, f1 + TT)
    RLO, RHI = slice(0, TH), slice(r1, r1 + TH)
    OF = slice(0, frames)
    first, last = slice(0, TT), slice(frames - TT, frames)
    rfirst, rlast = slice(0, TH), slice(rows - TH, rows)
    flast, ffirst = slice(frames, f1), slice(TT, 2 * TT)
    ROWS_ALL = slice(0, rows + 2 * TH)

    def plan(kind, c):
        return {
            Z_UP: ("ha", 1, own(OF, rlast, c), cells(F, RLO, c)),
            Z_DOWN: ("ha", -1, own(OF, rfirst, c), cells(F, RHI, c)),
            ZS_UP: ("ha", 1, strip(F, slice(rows, r1), c), strip(F, RLO, c)),
            ZS_DOWN: ("ha", -1, strip(F, slice(TH, 2 * TH), c), strip(F, RHI, c)),
            X_UP: ("ta", 1, own(last, slice(0, rows), c), cells(LO, R, c)),
            X_DOWN: ("ta", -1, own(first, slice(0, rows), c), cells(HI, R, c)),
            XLO_UP: ("ta", 1, cells(flast, RLO, c), cells(LO, RLO, c)),
            XLO_DOWN: ("ta", -1, cells(ffirst, RLO, c), cells(HI, RLO, c)),
            XHI_UP: ("ta", 1, cells(flast, RHI, c), cells(LO, RHI, c)),
            XHI_DOWN: ("ta", -1, cells(ffirst, RHI, c), cells(HI, RHI, c)),
            XS_UP: ("ta", 1, strip(flast, ROWS_ALL, c), strip(LO, ROWS_ALL, c)),
            XS_DOWN: ("ta", -1, strip(ffirst, ROWS_ALL, c), strip(HI, ROWS_ALL, c)),
        }[kind]

    def start(kind, c):
        axis, step, src, dst = plan(kind, c)
        sends = up if step == 1 else down

        @pl.when(sends[axis])
        def _():
            remote(kind, c, src, dst, {axis: at[axis] + step}).start()

    def got(kind, c):
        axis, step, _, dst = plan(kind, c)

        @pl.when((down if step == 1 else up)[axis])
        def _():
            pltpu.make_async_copy(dst, dst, recv_sem.at[kind, c]).wait()

    def sent(kind, c):
        axis, step, src, dst = plan(kind, c)

        @pl.when((up if step == 1 else down)[axis])
        def _():
            remote(kind, c, src, dst, {axis: at[axis] + step}).wait_send()

    def y_copy(c):
        return remote(Y_OWN, c, strip(OF, slice(0, rows), c, edge), strip(F, R, c), partner)

    ahead = 2
    for c in range(CHUNKS):
        y_copy(c).start()
    for c in range(CHUNKS + ahead):
        if c < CHUNKS:
            for kind in (Z_UP, Z_DOWN, X_UP, X_DOWN):
                start(kind, c)
        d = c - 1
        if 0 <= d < CHUNKS:
            y_copy(d).wait_recv()
            start(ZS_UP, d)
            start(ZS_DOWN, d)
        e = c - ahead
        if 0 <= e < CHUNKS:
            got(Z_UP, e)
            start(XLO_UP, e)
            start(XLO_DOWN, e)
            got(Z_DOWN, e)
            start(XHI_UP, e)
            start(XHI_DOWN, e)
            got(ZS_UP, e)
            got(ZS_DOWN, e)
            start(XS_UP, e)
            start(XS_DOWN, e)
    for c in range(CHUNKS):
        y_copy(c).wait_send()
        for kind in range(Z_UP, KINDS):
            sent(kind, c)
            if kind >= X_UP:
                got(kind, c)


def halo_call(mesh, qkv, edge):
    frames, rows, cols, channels = qkv.shape
    wide = edge.shape[-1]
    sizes = {axis: mesh.shape[axis] for axis in ("ta", "ha", "hd")}
    hbm = pl.BlockSpec(memory_space=pl.ANY)
    return pl.pallas_call(
        functools.partial(halo_kernel, sizes, channels - wide),
        in_specs=[hbm, hbm],
        out_specs=[hbm, hbm],
        out_shape=[
            jax.ShapeDtypeStruct((frames + 2 * TT, rows + 2 * TH, cols, wide), qkv.dtype),
            jax.ShapeDtypeStruct((frames + 2 * TT, (rows + 2 * TH) * TW, wide), qkv.dtype),
        ],
        scratch_shapes=[
            pltpu.SemaphoreType.DMA((KINDS, CHUNKS)),
            pltpu.SemaphoreType.DMA((KINDS, CHUNKS)),
        ],
        compiler_params=pltpu.CompilerParams(collective_id=0, has_side_effects=True),
    )(qkv, edge)


def column_shards(mesh, qkv, q_gain, k_gain, windows, frame_counts, row_counts):
    frames, rows, cols, channels = qkv.shape
    wide = channels // 3 * 2
    me = lax.axis_index("hd")
    zero = jnp.zeros((), jnp.int32)
    edge = lax.dynamic_slice(
        qkv, (zero, zero, jnp.where(me == 0, cols - TW, 0), zero + channels - wide), (frames, rows, TW, wide)
    ).reshape(frames, rows * TW, wide)
    ext, side = halo_call(mesh, qkv, edge)
    made = tables(frames, rows, cols, windows, frame_counts, row_counts)
    return attend_call(qkv, ext, side, *made, q_gain, k_gain)


def solution(mesh):
    def shards(qkv, *rest):
        fits = mesh.shape["hd"] == 2 and min(mesh.shape["ta"], mesh.shape["ha"]) > 1 and qkv.shape[2] % 16 == 0
        return column_shards(mesh, qkv, *rest) if fits else head_shards(qkv, *rest)

    return jax.shard_map(
        shards,
        mesh=mesh,
        in_specs=(P("ta", "ha", "hd", None), P(), P(), P("hd", None), P(), P()),
        out_specs=P("ta", "ha", "hd", None),
        check_vma=False,
    )
```
